1024 devices in a mesh: section: 16 (over z, y_lo), dp: 8 (over x), tensor: 8 (over y_hi, core).
Axes of the slice: x: 8, y: 8 (y_hi: 4, y_lo: 2; y = y_hi * 2 + y_lo), z: 8, core: 2. Of those that a mesh axis runs over, the one named last changes fastest.
Arguments:
- hidden: bfloat16 [16, 8, 256, 16384], P('section', 'dp', None, 'tensor'), may hold values from -80 to 80
- owner: int32 [16, 8, 256, 1], P('section', 'dp'), may hold values from 0 to 7; in each aligned block of 256 rows (0 to 255, 256 to 511, ..., all dimensions but the last counted through in order) at most 48 rows name the same one
- start: int32 [16, 8], P('section', 'dp'), may hold values from 0 to 1792
- live: int32 [16, 8], P('section', 'dp'), may hold values from 128 to 256
- norm_gain: float32 [16, 16384], P('section', 'tensor'), may hold values from 0.5 to 1.5
- w_kv: bfloat16 [16, 16384, 2048], P('section', 'tensor'), may hold values from -0.046875 to 0.046875
Outputs:
- kv_cache: bfloat16 [16, 8, 384, 2048], P('section', 'dp', None, 'tensor')
The draws below stay inside these ranges and needn't reach their ends.
Inputs may be any that keep to these rules, and one draw needn't show every extreme that they name: `owner`: among the 256 rows of one block no group is named by more than 48 rows, and some block names one group exactly 48 times. The live rows of a block are its first ones.
All inputs are finite; a program needn't handle non-finite values.
Results may differ from the reference program's by a relative error of at most 0.0049.
Values may be sent and summed in bfloat16 or wider, within the bound.
A program may use at most 64 MiB of HBM per device.

```python
import math
import jax
import jax.numpy as jnp
import numpy as np
from jax import lax

D = 16384
KVH = 8
HD = 128
PROMPT = 2048
TOK = 256
CAP = 48
SLOTS = 384
KVC = 2048
N_SECTION = 16
N_DP = 8


def draw_hidden(key, part):
    key_noise, key_rows, key_cols = jax.random.split(jax.random.fold_in(key, 11), 3)
    shape = (N_SECTION, N_DP, TOK, D)
    feature = jnp.arange(D, dtype=jnp.float32) / D
    col_scale = jnp.exp(jax.random.uniform(key_cols, (D,), jnp.float32, 0.0, math.log(2.5)))
    noise = jnp.clip(jax.random.normal(key_noise, shape, jnp.float32), -4.0, 4.0)
    rising = 3.0 ** feature
    row_scale = jnp.exp(jax.random.uniform(key_rows, (N_SECTION, N_DP, TOK, 1), jnp.float32, math.log(0.5), math.log(2.0)))
    return jnp.clip(noise * rising * col_scale * row_scale, -80.0, 80.0).astype(jnp.bfloat16)


def touch_ends(drawn, rng, low, largest):
    index_at = [jax.random.randint(jax.random.fold_in(rng, axis), (), 0, length) for axis, length in enumerate(drawn.shape)]
    main_axis = drawn.shape.index(max(drawn.shape))
    next_to = index_at[:main_axis] + [(index_at[main_axis] + 1) % drawn.shape[main_axis]] + index_at[main_axis + 1:]
    return drawn.at[tuple(index_at)].set(low).at[tuple(next_to)].set(largest)


def shard_levels(rng, shape, cuts, low, top_value):
    gain, own = 1.0, jax.random.fold_in(rng, 6)
    for dim, parts in cuts:
        steps = jnp.exp(jax.random.uniform(jax.random.fold_in(own, dim), (parts,), jnp.float32, low / len(cuts), top_value / len(cuts)))
        gain = gain * jnp.repeat(steps, shape[dim] // parts).reshape([-1 if axis == dim else 1 for axis in range(len(shape))])
    return gain


def shared_out(own_key, own, number, rows, number_of, top, most, skew):
    sequence = jax.random.permutation(own_key, number_of)
    packed, ordinary = shares(number_of, rows * top, most, skew, True), shares(number_of, rows * top, most, skew, False)
    places = jnp.arange(number_of)

    def named(lengths, turn):
        used = int((lengths > 0).sum())
        fixed = max(1, used // 4)
        passed = fixed + (places - fixed + turn * (used - fixed)) % max(1, number_of - fixed)
        return jnp.zeros((number_of,), jnp.int32).at[sequence[jnp.where(places < fixed, places, passed)]].set(jnp.asarray(lengths, jnp.int32))

    lengths = jnp.where(number % 4 == 0, named(packed, number // 4), named(ordinary, number - number // 4 - 1))
    mixed = jax.random.permutation(jax.random.fold_in(own, 3), number_of)
    giver, receiver = mixed[0:number_of // 2 * 2:2], mixed[1:number_of // 2 * 2:2]
    room = jnp.minimum(lengths[giver] - 1, most - lengths[receiver]) // 2
    room = jnp.where((giver == sequence[0]) | (receiver == sequence[0]) | (lengths[receiver] == 0), 0, jnp.maximum(room, 0))
    passed = jax.random.randint(jax.random.fold_in(own, 4), (number_of // 2,), 0, 1 << 20) % (room + 1)
    lengths = lengths.at[giver].add(-passed).at[receiver].add(passed)
    members = jnp.searchsorted(jnp.cumsum(lengths), jnp.arange(rows * top), side="right").astype(jnp.int32)
    grid = members.reshape(top, rows).T
    grid = grid[jax.random.permutation(jax.random.fold_in(own, 1), rows)]
    turn = jax.random.randint(jax.random.fold_in(own, 2), (rows, 1), 0, top)
    return jnp.take_along_axis(grid, (jnp.arange(top)[None, :] + turn) % top, axis=1)


def shares(count, total, bound, skew, full):
    portions = [(1 << 20) // math.isqrt(standing ** skew) + 1 for standing in range(1, count + 1)]
    largest = bound if full else min(bound, max(-(-total // count), total * portions[0] // sum(portions)))
    least = 1 if total - largest >= count - 1 else 0
    holding, surplus = [largest] + [least] * (count - 1), total - largest - least * (count - 1)
    while surplus > 0:
        free = [i for i in range(1, count) if holding[i] < largest] or [i for i in range(1, count) if holding[i] < bound]
        whole, remaining = sum([portions[i] for i in free]), surplus
        for i in free:
            more = min(bound - holding[i], max(1, remaining * portions[i] // whole), surplus)
            holding[i] = holding[i] + more
            surplus = surplus - more
    return np.array(holding)


def centred(key, shape, scale, reach, cuts=(), held_as=jnp.bfloat16):
    gain = shard_levels(key, shape, cuts, -0.22, 0.18) if cuts else 1.0
    drawn = jax.random.normal(key, shape, jnp.float32) * scale * gain
    return jnp.minimum(jnp.maximum(drawn, -reach), reach).astype(held_as)


def setup_inputs(seed: int = 0) -> dict:
    key_list = jax.random.split(jax.random.key(seed), 7)
    hidden = draw_hidden(jax.random.fold_in(key_list[6], 71), 0)
    owner_keys = jax.random.split(jax.random.fold_in(key_list[1], 1), N_SECTION * N_DP * TOK // TOK)
    owner_turns = jax.random.permutation(jax.random.fold_in(key_list[1], 3), N_SECTION * N_DP * TOK // TOK)
    owner = jax.vmap(lambda own, number: shared_out(jax.random.fold_in(key_list[1], 2), own, number, TOK, N_DP, 1, CAP, 2))(owner_keys, owner_turns).reshape((N_SECTION, N_DP, TOK, 1))
    start = touch_ends(jax.random.randint(key_list[2], (N_SECTION, N_DP), 0, PROMPT - TOK + 1), jax.random.fold_in(key_list[2], 1), 0, PROMPT - TOK).astype(jnp.int32)
    live = touch_ends(jax.random.randint(key_list[3], (N_SECTION, N_DP), TOK // 2, TOK + 1), jax.random.fold_in(key_list[3], 1), TOK // 2, TOK).astype(jnp.int32)
    norm_gain = jnp.clip(1.0 + 0.1 * jax.random.normal(key_list[4], (N_SECTION, D), jnp.float32), 0.5, 1.5)
    w_kv = centred(key_list[5], (N_SECTION, D, KVC), D ** -0.5, 0.046875, ((0, 16), (1, 8)))
    return {"hidden": hidden, "owner": owner, "start": start, "live": live, "norm_gain": norm_gain, "w_kv": w_kv}


EPSILON = 1e-05
ROPE_BASE = 500000.0

def rope_keys(kv_rows, positions):
    half_size = HD // 2
    inverse = ROPE_BASE ** (-(jnp.arange(half_size, dtype=jnp.float32) * 2.0 / HD))
    angles = positions.astype(jnp.float32)[:, None] * inverse[None, :]
    cosines = jnp.cos(angles)[:, None, :]
    sines = jnp.sin(angles)[:, None, :]
    key_part = kv_rows[:, :, 0, :]
    front_half = key_part[..., :half_size]
    back_half = key_part[..., half_size:]
    rotated = jnp.concatenate([front_half * cosines - back_half * sines, back_half * cosines + front_half * sines], axis=-1)
    return jnp.stack([rotated, kv_rows[:, :, 1, :]], axis=2)

def rank_in_group(target, row_alive):
    onehot = ((target[:, None] == jnp.arange(N_DP, dtype=jnp.int32)[None, :]) & row_alive[:, None]).astype(jnp.int32)
    earlier_hits = jnp.cumsum(onehot, axis=0).astype(jnp.int32) - onehot
    return lax.optimization_barrier(jnp.sum(earlier_hits * onehot, axis=1)).astype(jnp.int32)

def reference(hidden, owner, start, live, norm_gain, w_kv):

    def one_section(section_idx):
        earlier = jnp.maximum(section_idx - 1, 0).astype(jnp.int32)
        tok_rows = hidden[earlier]
        widened = tok_rows.astype(jnp.float32)
        mean_sq = lax.optimization_barrier(jnp.mean(widened * widened, axis=-1, keepdims=True))
        normed = (widened * norm_gain[section_idx] * lax.rsqrt(mean_sq + EPSILON)).astype(jnp.bfloat16)
        kv_rows = jnp.dot(normed.reshape(N_DP * TOK, D), w_kv[section_idx], preferred_element_type=jnp.float32)
        row_index = jnp.arange(TOK, dtype=jnp.int32)
        positions = (start[earlier][:, None] + row_index[None, :]).reshape(-1).astype(jnp.int32)
        kv_rows = rope_keys(kv_rows.reshape(N_DP * TOK, KVH, 2, HD), positions)
        kv_rows = kv_rows.reshape(N_DP * TOK, KVC).astype(jnp.bfloat16)
        target = owner[earlier][:, :, 0].astype(jnp.int32)
        row_alive = row_index[None, :] < live[earlier][:, None]
        rank_in = jax.vmap(rank_in_group)(target, row_alive)
        target_group = jnp.where(row_alive, target, N_DP).astype(jnp.int32)
        target_slot = (jnp.arange(N_DP, dtype=jnp.int32)[:, None] * CAP + rank_in).astype(jnp.int32)
        sectioned = jnp.zeros((N_DP, SLOTS, KVC), jnp.bfloat16)
        sectioned = sectioned.at[target_group.reshape(-1), target_slot.reshape(-1)].set(kv_rows, mode='drop')
        return jnp.where(section_idx > 0, sectioned, jnp.zeros_like(sectioned))
    return lax.map(one_section, jnp.arange(N_SECTION, dtype=jnp.int32))
```

```python
import functools
import math

import jax
import jax.numpy as jnp
import numpy as np
from jax import lax
from jax.experimental import pallas as pl
from jax.experimental.pallas import tpu as pltpu
from jax.sharding import PartitionSpec as P

HD = 128
EPSILON = 1e-05
ROPE_BASE = 500000.0
F32 = jnp.float32
BF16 = jnp.bfloat16
I32 = jnp.int32


def feature_chunks(width):
    quarter = width // 4
    if quarter % 256:
        return [(0, width // 2), (width // 2, width // 2)]
    cuts = [quarter, quarter, quarter, quarter // 2, quarter // 2]
    return [(sum(cuts[:i]), cut) for i, cut in enumerate(cuts)]


def dot(a, b):
    return jnp.dot(a, b, preferred_element_type=F32)


def kernel(
    sizes,
    hidden,
    owner,
    start,
    live,
    gain,
    inverse,
    weight,
    out,
    own_rows,
    rows,
    w_vmem,
    total,
    ssq_out,
    ssq_in,
    meta_out,
    meta_in,
    scale_ref,
    cos_ref,
    sin_ref,
    place_ref,
    pair_out,
    pair_in,
    hop_out,
    hop_in,
    late_ref,
    packed,
    local_sem,
    shift_sem,
    ssq_sem,
    meta_sem,
    pair_sem,
    hop_sem,
    route_sem,
    keep_sem,
):
    n_section, n_dp, n_tensor, d_model = sizes
    n_ring = n_tensor // 2
    tok, width = own_rows.shape
    slots = place_ref.shape[0]
    cap = slots // n_dp
    half = tok // 2
    chunks = feature_chunks(width)
    sec, dp, ten = lax.axis_index("section"), lax.axis_index("dp"), lax.axis_index("tensor")
    ring, core = ten // 2, ten % 2
    after = (sec + 1) % n_section
    before = (sec + n_section - 1) % n_section
    sibling = (sec, dp, ring * 2 + 1 - core)
    right = (sec, dp, ((ring + 1) % n_ring) * 2 + core)
    left = (sec, dp, ((ring + n_ring - 1) % n_ring) * 2 + core)

    def remote(src, dst, sems, index, device, arrive=None):
        index = index if isinstance(index, tuple) else (index,)
        arrive = index if arrive is None else arrive
        return pltpu.make_async_remote_copy(
            src_ref=src,
            dst_ref=dst,
            send_sem=sems.at[(0, *index)],
            recv_sem=sems.at[(1, *arrive)],
            device_id=device,
            device_id_type=pl.DeviceIdType.MESH,
        )

    barrier = pltpu.get_barrier_semaphore()
    greeted = [(before, dp, t) for t in range(n_tensor)] + [sibling, right, left]
    greeted += [(sec, (dp + k) % n_dp, ten) for k in range(1, n_dp)]
    for device in greeted:
        pl.semaphore_signal(barrier, inc=1, device_id=device, device_id_type=pl.DeviceIdType.MESH)

    take_rows = pltpu.make_async_copy(hidden.at[0, 0], own_rows, local_sem.at[0])
    take_rows.start()
    take_w = []
    for j, (at, wide) in enumerate(chunks):
        part = pl.ds(at, wide)
        take_w.append(
            pltpu.make_async_copy(weight.at[0, part], w_vmem.at[part], local_sem.at[1 + j])
        )
        take_w[-1].start()

    row_id = lax.broadcasted_iota(I32, (8, tok), 0)
    meta_out[...] = jnp.where(row_id == 0, owner[...], jnp.where(row_id == 1, start[0, 0], live[0, 0]))
    pl.semaphore_wait(barrier, len(greeted))

    shifts = []
    for j, (at, wide) in enumerate(chunks):
        part = pl.ds(at, wide)
        shifts.append(
            remote(hidden.at[0, 0, :, part], rows.at[:, part], shift_sem, j, (after, dp, ten))
        )
        shifts[-1].start()
    send_meta = remote(meta_out, meta_in, meta_sem, 0, (after, dp, ten))
    send_meta.start()

    take_rows.wait()
    squares = jnp.zeros((tok, HD), F32)
    for k in range(width // HD):
        piece = own_rows[:, k * HD : (k + 1) * HD].astype(F32)
        squares = squares + piece * piece
    ssq_out[...] = jnp.sum(squares.T, axis=0, keepdims=True)
    send_ssq = []
    for k in range(n_tensor):
        send_ssq.append(remote(ssq_out, ssq_in.at[ten], ssq_sem, k, (after, dp, k), (ten,)))
        send_ssq[-1].start()

    send_meta.wait_recv()
    own_row = meta_in[0:1, :]
    alive = lax.broadcasted_iota(I32, (1, tok), 1) < jnp.where(sec > 0, meta_in[2:3, :], 0)
    named = (lax.broadcasted_iota(I32, (16, tok), 0) == own_row) & alive
    named = jnp.where(named, 1.0, 0.0)
    earlier = lax.broadcasted_iota(I32, (tok, tok), 0) < lax.broadcasted_iota(I32, (tok, tok), 1)
    ranks = dot(named.astype(BF16), jnp.where(earlier, 1.0, 0.0).astype(BF16))
    rank = jnp.sum(ranks * named, axis=0, keepdims=True).astype(I32)
    slot = jnp.where(alive, own_row * cap + rank, slots)
    placing = lax.broadcasted_iota(I32, (slots, tok), 0) == slot
    place_ref[...] = jnp.where(placing, 1.0, 0.0).astype(BF16)
    position = lax.broadcasted_iota(I32, (tok, HD), 0) + meta_in[1:2, :HD]
    angle = position.astype(F32) * inverse[...]
    cos_ref[...] = jnp.cos(angle)
    front = lax.broadcasted_iota(I32, (tok, HD), 1) < HD // 2
    sine = jnp.sin(angle)
    sin_ref[...] = jnp.where(front, -sine, sine)

    for k in range(n_tensor):
        remote(ssq_out, ssq_in.at[k], ssq_sem, k, (after, dp, ten)).wait_recv()
    sum_sq = ssq_in[0]
    for k in range(1, n_tensor):
        sum_sq = sum_sq + ssq_in[k]
    scale = lax.rsqrt(sum_sq / d_model + EPSILON)
    scale_ref[...] = jnp.broadcast_to(scale, (HD, tok)).T

    def normed(at, wide):
        pieces = []
        for k in range(at, at + wide, HD):
            piece = rows[:, k : k + HD].astype(F32) * gain[:, k : k + HD] * scale_ref[...]
            pieces.append(piece.astype(BF16))
        return jnp.concatenate(pieces, axis=1)

    for j, (at, wide) in enumerate(chunks[:-1]):
        shifts[j].wait_recv()
        take_w[j].wait()
        activation = normed(at, wide)
        for n in range(0, total.shape[1], 256):
            product = dot(activation, w_vmem[at : at + wide, n : n + 256])
            total[:, n : n + 256] = product if j == 0 else total[:, n : n + 256] + product

    at, wide = chunks[-1]
    shifts[-1].wait_recv()
    take_w[-1].wait()
    activation = normed(at, wide)
    for n in range(n_ring):
        cols = pl.ds(pl.multiple_of((n * 2 + 1 - core) * 256, 256), 256)
        done = (total[:, cols] + dot(activation, w_vmem[at : at + wide, cols])).astype(BF16)
        pair_out[0, n] = done[:, :HD]
        pair_out[1, n] = done[:, HD:]
    to_pair = [remote(pair_out.at[g], pair_in.at[g], pair_sem, g, sibling) for g in range(2)]
    to_pair[0].start()
    to_pair[1].start()
    for n in range(n_ring):
        cols = pl.ds(pl.multiple_of((n * 2 + core) * 256, 256), 256)
        total[:, cols] += dot(activation, w_vmem[at : at + wide, cols])

    top, low = slice(0, half), slice(half, tok)

    def chip_sum(g, there):
        there = there % n_ring
        cols = pl.ds(pl.multiple_of((there * 2 + core) * 256 + g * HD, HD), HD)
        return total[:, cols] + pair_in[g, there].astype(F32)

    def hop(g, i, device):
        return remote(hop_out.at[g, i], hop_in.at[g, i], hop_sem, (g, i), device)

    for g in range(2):
        to_pair[g].wait_recv()
        across = chip_sum(g, ring + 2)
        hop_out[g, 0] = across[top].astype(BF16)
        hop_out[g, 1] = across[low].astype(BF16)
        hop(g, 0, right).start()
        hop(g, 1, left).start()
        to_right = chip_sum(g, ring + 1)
        hop_out[g, 2] = to_right[low].astype(BF16)
        hop(g, 2, right).start()
        late_ref[g, 0] = to_right[top]
        to_left = chip_sum(g, ring + n_ring - 1)
        hop_out[g, 3] = to_left[top].astype(BF16)
        hop(g, 3, left).start()
        late_ref[g, 1] = to_left[low]
    for g in range(2):
        hop(g, 0, right).wait_recv()
        hop_out[g, 4] = (late_ref[g, 0] + hop_in[g, 0].astype(F32)).astype(BF16)
        hop(g, 4, right).start()
        hop(g, 1, left).wait_recv()
        hop_out[g, 5] = (late_ref[g, 1] + hop_in[g, 1].astype(F32)).astype(BF16)
        hop(g, 5, left).start()

    keeps, routes = [], []
    for g in range(2):
        mine = chip_sum(g, ring)
        hop(g, 2, right).wait_recv()
        hop(g, 3, left).wait_recv()
        hop(g, 4, right).wait_recv()
        hop(g, 5, left).wait_recv()
        upper = mine[top] + hop_in[g, 4].astype(F32) + hop_in[g, 3].astype(F32)
        lower = mine[low] + hop_in[g, 2].astype(F32) + hop_in[g, 5].astype(F32)
        finished = jnp.concatenate([upper, lower], axis=0)
        if g == 0:
            finished = finished * cos_ref[...] + pltpu.roll(finished, HD // 2, 1) * sin_ref[...]
        packed[g] = dot(place_ref[...], finished.astype(BF16)).astype(BF16)
        cols = pl.ds(g * HD, HD)

        def slot_rows(group):
            return pl.ds(pl.multiple_of(group * cap, 16), cap)

        for k in sorted(range(1, n_dp), key=lambda k: -min(k, n_dp - k)):
            peer = (dp + k) % n_dp
            routes.append(
                remote(
                    packed.at[g, slot_rows(peer)],
                    out.at[0, 0, slot_rows(dp), cols],
                    route_sem,
                    (g, k),
                    (sec, peer, ten),
                )
            )
            routes[-1].start()
        keeps.append(
            pltpu.make_async_copy(
                packed.at[g, slot_rows(dp)], out.at[0, 0, slot_rows(dp), cols], keep_sem.at[g]
            )
        )
        keeps[-1].start()

    for copy in routes:
        copy.wait_recv()
    for copy in [*shifts, send_meta, *send_ssq, *to_pair, *routes]:
        copy.wait_send()
    for g in range(2):
        for i in range(6):
            hop(g, i, right).wait_send()
    for copy in keeps:
        copy.wait()


def per_device(sizes, hidden, owner, start, live, norm_gain, w_kv):
    n_section, n_dp, n_tensor, d_model = sizes
    tok, width = hidden.shape[2:]
    columns = w_kv.shape[2]
    slots = (3 * tok // (2 * n_dp)) * n_dp
    local_cols = columns // n_tensor
    exponent = np.arange(HD // 2, dtype=np.float32) * np.float32(2.0) / np.float32(HD)
    inverse = np.power(np.float32(ROPE_BASE), -exponent).astype(np.float32)
    inverse = jnp.asarray(np.concatenate([inverse, inverse])[None, :])
    n_chunks = len(feature_chunks(width))
    vmem, smem, anywhere = (
        pl.BlockSpec(memory_space=pltpu.VMEM),
        pl.BlockSpec(memory_space=pltpu.SMEM),
        pl.BlockSpec(memory_space=pl.ANY),
    )
    half = tok // 2
    n_ring = n_tensor // 2
    dma = pltpu.SemaphoreType.DMA
    return pl.pallas_call(
        functools.partial(kernel, sizes),
        out_shape=jax.ShapeDtypeStruct((1, 1, slots, local_cols), BF16),
        in_specs=[anywhere, vmem, smem, smem, vmem, vmem, anywhere],
        out_specs=anywhere,
        scratch_shapes=[
            pltpu.VMEM((tok, width), BF16),
            pltpu.VMEM((tok, width), BF16),
            pltpu.VMEM((width, columns), BF16),
            pltpu.VMEM((tok, columns), F32),
            pltpu.VMEM((1, tok), F32),
            pltpu.VMEM((n_tensor, 1, tok), F32),
            pltpu.VMEM((8, tok), I32),
            pltpu.VMEM((8, tok), I32),
            pltpu.VMEM((tok, HD), F32),
            pltpu.VMEM((tok, HD), F32),
            pltpu.VMEM((tok, HD), F32),
            pltpu.VMEM((slots, tok), BF16),
            pltpu.VMEM((2, n_ring, tok, HD), BF16),
            pltpu.VMEM((2, n_ring, tok, HD), BF16),
            pltpu.VMEM((2, 6, half, HD), BF16),
            pltpu.VMEM((2, 6, half, HD), BF16),
            pltpu.VMEM((2, 2, half, HD), F32),
            pltpu.VMEM((2, slots, HD), BF16),
            dma((1 + n_chunks,)),
            dma((2, n_chunks)),
            dma((2, n_tensor)),
            dma((2, 1)),
            dma((2, 2)),
            dma((2, 2, 6)),
            dma((2, 2, n_dp)),
            dma((2,)),
        ],
        compiler_params=pltpu.CompilerParams(
            collective_id=0, has_side_effects=True, vmem_limit_bytes=32 * 2**20
        ),
        cost_estimate=pl.CostEstimate(
            flops=2 * tok * width * columns,
            bytes_accessed=2 * width * (columns + 2 * tok),
            transcendentals=2 * tok * HD,
        ),
    )(hidden, owner.reshape(1, tok), start, live, norm_gain, inverse, w_kv)


def solution(mesh):
    sizes = (mesh.shape["section"], mesh.shape["dp"], mesh.shape["tensor"])
    in_specs = (
        P("section", "dp", None, "tensor"),
        P("section", "dp", None, None),
        P("section", "dp"),
        P("section", "dp"),
        P("section", "tensor"),
        P("section", "tensor", None),
    )
    out_specs = P("section", "dp", None, "tensor")

    def run(hidden, owner, start, live, norm_gain, w_kv):
        body = functools.partial(per_device, (*sizes, hidden.shape[3]))
        return jax.shard_map(
            body, mesh=mesh, in_specs=in_specs, out_specs=out_specs, check_vma=False
        )(hidden, owner, start, live, norm_gain, w_kv)

    return run
```

```python
import functools

import jax
import jax.numpy as jnp
import numpy as np
from jax import lax
from jax.experimental import pallas as pl
from jax.experimental.pallas import tpu as pltpu
from jax.sharding import PartitionSpec as P

HD = 128
EPSILON = 1e-05
ROPE_BASE = 500000.0
F32 = jnp.float32
BF16 = jnp.bfloat16
I32 = jnp.int32


GROUPS = ((256, 8),)
LAST_COLUMNS = 2


def units_of(groups, columns):
    units = [(q, 0, columns) for q in range(len(groups) - 1)]
    wide = columns // LAST_COLUMNS
    return units + [(len(groups) - 1, i * wide, wide) for i in range(LAST_COLUMNS)]


def pieces_of(groups, width):
    pieces, row = [], 0
    for q, (count, cuts) in enumerate(groups):
        wide = width // cuts
        pieces += [(q, row, count, i * wide, wide) for i in range(cuts)]
        row += count
    return pieces


def dot(a, b):
    return jnp.dot(a, b, preferred_element_type=F32)


def kernel(
    sizes,
    hidden,
    owner,
    start,
    live,
    gain,
    inverse,
    weight,
    out,
    own_rows,
    owner_vmem,
    gain_vmem,
    inverse_vmem,
    rows,
    w_vmem,
    total,
    ssq_out,
    ssq_in,
    meta_out,
    meta_in,
    scale_ref,
    cos_ref,
    sin_ref,
    place_ref,
    pair_out,
    pair_in,
    hop_out,
    hop_in,
    late_ref,
    slot_total,
    packed,
    local_sem,
    shift_sem,
    ssq_sem,
    meta_sem,
    pair_sem,
    hop_sem,
    route_sem,
    keep_sem,
):
    n_section, n_dp, n_tensor, d_model = sizes
    n_ring = n_tensor // 2
    tok, width = own_rows.shape
    slots, columns = packed.shape
    cap = slots // n_dp
    pieces = pieces_of(GROUPS, width)
    units = units_of(GROUPS, columns)
    first_row = [sum(count for count, _ in GROUPS[:q]) for q in range(len(GROUPS))]
    sec, dp, ten = lax.axis_index("section"), lax.axis_index("dp"), lax.axis_index("tensor")
    ring, core = ten // 2, ten % 2
    after = (sec + 1) % n_section
    before = (sec + n_section - 1) % n_section
    sends, takes = sec < n_section - 1, sec > 0
    sibling = (sec, dp, ring * 2 + 1 - core)
    right = (sec, dp, ((ring + 1) % n_ring) * 2 + core)
    left = (sec, dp, ((ring + n_ring - 1) % n_ring) * 2 + core)
    peers = [(sec, (dp + k) % n_dp, ten) for k in range(1, n_dp)]

    def remote(src, dst, sems, index, device, arrive=None):
        index = index if isinstance(index, tuple) else (index,)
        arrive = index if arrive is None else arrive
        return pltpu.make_async_remote_copy(
            src_ref=src,
            dst_ref=dst,
            send_sem=sems.at[(0, *index)],
            recv_sem=sems.at[(1, *arrive)],
            device_id=device,
            device_id_type=pl.DeviceIdType.MESH,
        )

    def shift(i):
        _, row, count, at, wide = pieces[i]
        here = (pl.ds(row, count), pl.ds(at, wide))
        return remote(hidden.at[(0, 0, *here)], rows.at[here], shift_sem, i, (after, dp, ten))

    def send_meta():
        return remote(meta_out, meta_in, meta_sem, 0, (after, dp, ten))

    def send_ssq(k):
        return remote(ssq_out, ssq_in.at[ten], ssq_sem, k, (after, dp, k), (ten,))

    def take(i):
        pairs = [(owner, owner_vmem), (hidden.at[0, 0], own_rows), (gain, gain_vmem), (inverse, inverse_vmem)]
        pairs.append((weight.at[0], w_vmem))
        return pltpu.make_async_copy(*pairs[i], local_sem.at[i])

    barrier = pltpu.get_barrier_semaphore()

    def greet(devices):
        for device in devices:
            pl.semaphore_signal(
                barrier, inc=1, device_id=device, device_id_type=pl.DeviceIdType.MESH
            )

    @pl.when(takes)
    def _():
        greet([(before, dp, t) for t in range(n_tensor)])
        greet([sibling, right, left, *peers])

    @pl.when(sends)
    def _():
        take(0).start()
        take(1).start()

    @pl.when(takes)
    def _():
        for i in (2, 3, 4):
            take(i).start()

    @pl.when(sec == 0)
    def _():
        packed[...] = jnp.zeros_like(packed)
        pltpu.make_async_copy(packed, out.at[0, 0], keep_sem.at[0]).start()

    @pl.when(sends)
    def _():
        take(0).wait()
        row_id = lax.broadcasted_iota(I32, (8, tok), 0)
        meta_out[...] = jnp.where(
            row_id == 0, owner_vmem[...], jnp.where(row_id == 1, start[0, 0], live[0, 0])
        )

    within = 3 + len(peers)

    @pl.when(sends & takes)
    def _():
        pl.semaphore_wait(barrier, n_tensor + within)

    @pl.when(sec == 0)
    def _():
        pl.semaphore_wait(barrier, n_tensor)

    @pl.when(sec == n_section - 1)
    def _():
        pl.semaphore_wait(barrier, within)

    @pl.when(sends)
    def _():
        send_meta().start()
        shift(0).start()
        take(1).wait()
        squares = jnp.zeros((tok, HD), F32)
        for k in range(width // HD):
            piece = own_rows[:, k * HD : (k + 1) * HD].astype(F32)
            squares = squares + piece * piece
        ssq_out[...] = jnp.sum(squares.T, axis=0, keepdims=True)
        for k in range(n_tensor):
            send_ssq(k).start()
        for i in range(1, len(pieces)):
            shift(i).start()

    def prepare():
        send_meta().wait_recv()
        own_row = meta_in[0:1, :]
        alive = lax.broadcasted_iota(I32, (1, tok), 1) < meta_in[2:3, :]
        named = (lax.broadcasted_iota(I32, (16, tok), 0) == own_row) & alive
        named = jnp.where(named, 1.0, 0.0)
        row_at = lax.broadcasted_iota(I32, (tok, tok), 0)
        earlier = row_at < lax.broadcasted_iota(I32, (tok, tok), 1)
        ranks = dot(named.astype(BF16), jnp.where(earlier, 1.0, 0.0).astype(BF16))
        rank = jnp.sum(ranks * named, axis=0, keepdims=True).astype(I32)
        slot = jnp.where(alive, own_row * cap + rank, slots)
        placing = lax.broadcasted_iota(I32, (slots, tok), 0) == slot
        placing = jnp.where(placing, 1.0, 0.0).astype(BF16)
        for q, (count, _) in enumerate(GROUPS):
            place_ref[q, :, :count] = placing[:, first_row[q] : first_row[q] + count]
        position = lax.broadcasted_iota(I32, (tok, HD), 0) + meta_in[1:2, :HD]
        take(3).wait()
        take(2).wait()
        angle = position.astype(F32) * inverse_vmem[...]
        cos_ref[...] = jnp.cos(angle)
        front = lax.broadcasted_iota(I32, (tok, HD), 1) < HD // 2
        sine = jnp.sin(angle)
        sin_ref[...] = jnp.where(front, -sine, sine)
        for k in range(n_tensor):
            remote(ssq_out, ssq_in.at[k], ssq_sem, k, (after, dp, ten)).wait_recv()
        sum_sq = ssq_in[0]
        for k in range(1, n_tensor):
            sum_sq = sum_sq + ssq_in[k]
        scale = lax.rsqrt(sum_sq / d_model + EPSILON)
        scale_ref[...] = jnp.broadcast_to(scale, (HD, tok)).T

    def normed(row, count, at, wide):
        here = slice(row, row + count)
        scale = scale_ref[here]
        parts = []
        for k in range(at, at + wide, HD):
            part = rows[here, k : k + HD].astype(F32) * gain_vmem[:, k : k + HD] * scale
            parts.append(part.astype(BF16))
        return jnp.concatenate(parts, axis=1)

    def pair(q):
        here = pl.ds(first_row[q], GROUPS[q][0])
        return remote(pair_out.at[:, here], pair_in.at[:, here], pair_sem, q, sibling)

    def project(q):
        mine = [(i, p) for i, p in enumerate(pieces) if p[0] == q]
        for i, (_, row, count, at, wide) in mine:
            here = slice(row, row + count)
            shift(i).wait_recv()
            if i == 0:
                take(4).wait()
            activation = normed(row, count, at, wide)
            if i != mine[-1][0]:
                for n in range(0, total.shape[1], columns):
                    cols = slice(n, n + columns)
                    product = dot(activation, w_vmem[at : at + wide, cols])
                    total[here, cols] = product if at == 0 else total[here, cols] + product
                continue
            for side in (1 - core, core):
                for n in range(n_ring):
                    cols = pl.ds(pl.multiple_of((n * 2 + side) * columns, columns), columns)
                    product = dot(activation, w_vmem[at : at + wide, cols])
                    if at:
                        product = total[here, cols] + product
                    if side is core:
                        total[here, cols] = product
                    else:
                        pair_out[n, here] = product.astype(BF16)
                if side is not core:
                    pair(q).start()

    def rows_of(q):
        row, count = first_row[q], GROUPS[q][0]
        return row, row + count // 2, row + count

    def chip_sum(u, there, first, last):
        _, at, wide = units[u]
        there = there % n_ring
        cols = pl.ds(pl.multiple_of((there * 2 + core) * columns + at, HD), wide)
        here = slice(first, last)
        return total[here, cols] + pair_in[there, here, at : at + wide].astype(F32)

    def view(u):
        q, at, wide = units[u]
        return slice(first_row[q] // 2, (first_row[q] + GROUPS[q][0]) // 2), slice(at, at + wide)

    def hop(u, i, device):
        r, c = view(u)
        here = (i, pl.ds(r.start, r.stop - r.start), pl.ds(c.start, c.stop - c.start))
        return remote(hop_out.at[here], hop_in.at[here], hop_sem, (u, i), device)

    def across(u):
        a, b, c = rows_of(units[u][0])
        r, cols = view(u)
        hop_out[0, r, cols] = chip_sum(u, ring + 2, a, b).astype(BF16)
        hop(u, 0, right).start()
        hop_out[1, r, cols] = chip_sum(u, ring + 2, b, c).astype(BF16)
        hop(u, 1, left).start()
        hop_out[2, r, cols] = chip_sum(u, ring + 1, b, c).astype(BF16)
        hop(u, 2, right).start()
        hop_out[3, r, cols] = chip_sum(u, ring + n_ring - 1, a, b).astype(BF16)
        hop(u, 3, left).start()
        late_ref[0, r, cols] = chip_sum(u, ring + 1, a, b)
        late_ref[1, r, cols] = chip_sum(u, ring + n_ring - 1, b, c)

    def relay(u):
        r, cols = view(u)
        for side, device in ((0, right), (1, left)):
            hop(u, side, device).wait_recv()
            both = late_ref[side, r, cols] + hop_in[side, r, cols].astype(F32)
            hop_out[4 + side, r, cols] = both.astype(BF16)
            hop(u, 4 + side, device).start()

    def slot_rows(group):
        return pl.ds(pl.multiple_of(group * cap, 16), cap)

    def route(g, k):
        cols = pl.ds(g * HD, HD)
        peer = (dp + k) % n_dp
        return remote(
            packed.at[slot_rows(peer), cols],
            out.at[0, 0, slot_rows(dp), cols],
            route_sem,
            (g, k),
            (sec, peer, ten),
        )

    def keep(g):
        cols = pl.ds(g * HD, HD)
        return pltpu.make_async_copy(
            packed.at[slot_rows(dp), cols], out.at[0, 0, slot_rows(dp), cols], keep_sem.at[g]
        )

    def finish(u):
        q, at, wide = units[u]
        a, b, c = rows_of(q)
        r, cols = view(u)
        mine = chip_sum(u, ring, a, c)
        for i in (2, 3, 4, 5):
            hop(u, i, right).wait_recv()
        upper = hop_in[4, r, cols].astype(F32) + hop_in[3, r, cols].astype(F32)
        lower = hop_in[2, r, cols].astype(F32) + hop_in[5, r, cols].astype(F32)
        rows_done = mine + jnp.concatenate([upper, lower], axis=0)
        for k in range(0, wide, HD):
            part = rows_done[:, k : k + HD]
            g = (at + k) // HD
            if g % 2 == 0:
                part = part * cos_ref[a:c] + pltpu.roll(part, HD // 2, 1) * sin_ref[a:c]
            put = dot(place_ref[q, :, : c - a], part.astype(BF16))
            there = slice(g * HD, (g + 1) * HD)
            if q:
                put = slot_total[:, there] + put
            if q < len(GROUPS) - 1:
                slot_total[:, there] = put
                continue
            packed[:, there] = put.astype(BF16)
            for k in routed:
                route(g, k).start()
            keep(g).start()

    routed = sorted(range(1, n_dp), key=lambda k: -min(k, n_dp - k))

    @pl.when(takes)
    def _():
        prepare()
        for q in range(len(GROUPS)):
            project(q)
            now = [u for u, unit in enumerate(units) if unit[0] == q]
            pair(q).wait_recv()
            for u in now:
                across(u)
            for u, unit in enumerate(units):
                if unit[0] == q - 1:
                    finish(u)
            for u in now:
                relay(u)
        for u in now:
            finish(u)
        for g in range(columns // HD):
            for k in routed:
                route(g, k).wait_recv()
        for g in range(columns // HD):
            for k in routed:
                route(g, k).wait_send()
            keep(g).wait()
        for q in range(len(GROUPS)):
            pair(q).wait_send()
        for u in range(len(units)):
            for i in range(6):
                hop(u, i, right).wait_send()

    @pl.when(sends)
    def _():
        for i in range(len(pieces)):
            shift(i).wait_send()
        send_meta().wait_send()
        for k in range(n_tensor):
            send_ssq(k).wait_send()

    @pl.when(sec == 0)
    def _():
        pltpu.make_async_copy(packed, out.at[0, 0], keep_sem.at[0]).wait()


def per_device(sizes, hidden, owner, start, live, norm_gain, w_kv):
    n_section, n_dp, n_tensor, d_model = sizes
    tok, width = hidden.shape[2:]
    columns = w_kv.shape[2]
    slots = (3 * tok // (2 * n_dp)) * n_dp
    local_cols = columns // n_tensor
    exponent = np.arange(HD // 2, dtype=np.float32) * np.float32(2.0) / np.float32(HD)
    inverse = np.power(np.float32(ROPE_BASE), -exponent).astype(np.float32)
    inverse = jnp.asarray(np.concatenate([inverse, inverse])[None, :])
    smem = pl.BlockSpec(memory_space=pltpu.SMEM)
    hbm = pl.BlockSpec(memory_space=pltpu.HBM)
    half = tok // 2
    n_ring = n_tensor // 2
    most = max(count for count, _ in GROUPS)
    n_units = len(units_of(GROUPS, local_cols))
    dma = pltpu.SemaphoreType.DMA
    return pl.pallas_call(
        functools.partial(kernel, sizes),
        out_shape=jax.ShapeDtypeStruct((1, 1, slots, local_cols), BF16),
        in_specs=[hbm, hbm, smem, smem, hbm, hbm, hbm],
        out_specs=hbm,
        scratch_shapes=[
            pltpu.VMEM((tok, width), BF16),
            pltpu.VMEM((1, tok), I32),
            pltpu.VMEM((1, width), F32),
            pltpu.VMEM((1, HD), F32),
            pltpu.VMEM((tok, width), BF16),
            pltpu.VMEM((width, columns), BF16),
            pltpu.VMEM((tok, columns), F32),
            pltpu.VMEM((1, tok), F32),
            pltpu.VMEM((n_tensor, 1, tok), F32),
            pltpu.VMEM((8, tok), I32),
            pltpu.VMEM((8, tok), I32),
            pltpu.VMEM((tok, HD), F32),
            pltpu.VMEM((tok, HD), F32),
            pltpu.VMEM((tok, HD), F32),
            pltpu.VMEM((len(GROUPS), slots, most), BF16),
            pltpu.VMEM((n_ring, tok, local_cols), BF16),
            pltpu.VMEM((n_ring, tok, local_cols), BF16),
            pltpu.VMEM((6, half, local_cols), BF16),
            pltpu.VMEM((6, half, local_cols), BF16),
            pltpu.VMEM((2, half, local_cols), F32),
            pltpu.VMEM((slots, local_cols), F32),
            pltpu.VMEM((slots, local_cols), BF16),
            dma((5,)),
            dma((2, len(pieces_of(GROUPS, width)))),
            dma((2, n_tensor)),
            dma((2, 1)),
            dma((2, len(GROUPS))),
            dma((2, n_units, 6)),
            dma((2, local_cols // HD, n_dp)),
            dma((local_cols // HD,)),
        ],
        compiler_params=pltpu.CompilerParams(
            collective_id=0, has_side_effects=True, vmem_limit_bytes=60 * 2**20
        ),
        cost_estimate=pl.CostEstimate(
            flops=2 * tok * width * columns,
            bytes_accessed=2 * width * (columns + 2 * tok),
            transcendentals=2 * tok * HD,
        ),
    )(hidden, owner.reshape(1, tok), start, live, norm_gain, inverse, w_kv)


def solution(mesh):
    sizes = (mesh.shape["section"], mesh.shape["dp"], mesh.shape["tensor"])
    in_specs = (
        P("section", "dp", None, "tensor"),
        P("section", "dp", None, None),
        P("section", "dp"),
        P("section", "dp"),
        P("section", "tensor"),
        P("section", "tensor", None),
    )
    out_specs = P("section", "dp", None, "tensor")

    def run(hidden, owner, start, live, norm_gain, w_kv):
        body = functools.partial(per_device, (*sizes, hidden.shape[3]))
        return jax.shard_map(
            body, mesh=mesh, in_specs=in_specs, out_specs=out_specs, check_vma=False
        )(hidden, owner, start, live, norm_gain, w_kv)

    return run
```

```python
import functools

import jax
import jax.numpy as jnp
import numpy as np
from jax import lax
from jax.experimental import pallas as pl
from jax.experimental.pallas import tpu as pltpu
from jax.sharding import PartitionSpec as P

HD = 128
EPSILON = 1e-05
ROPE_BASE = 500000.0
F32 = jnp.float32
BF16 = jnp.bfloat16
I32 = jnp.int32


PIECES = 8


def feature_pieces(width):
    count = min(PIECES, width // HD)
    wide = width // count
    return [(i * wide, wide) for i in range(count)]


def dot(a, b):
    return jnp.dot(a, b, preferred_element_type=F32)


def kernel(
    sizes,
    hidden,
    owner,
    start,
    live,
    gain,
    inverse,
    weight,
    out,
    own_rows,
    owner_vmem,
    gain_vmem,
    inverse_vmem,
    rows,
    w_vmem,
    total,
    ssq_out,
    ssq_in,
    meta_out,
    meta_in,
    scale_ref,
    cos_ref,
    sin_ref,
    place_ref,
    pair_out,
    pair_in,
    hop_out,
    hop_in,
    late_ref,
    packed,
    local_sem,
    shift_sem,
    ssq_sem,
    meta_sem,
    pair_sem,
    hop_sem,
    route_sem,
    keep_sem,
):
    n_section, n_dp, n_tensor, d_model = sizes
    n_ring = n_tensor // 2
    tok, width = own_rows.shape
    slots, columns = packed.shape
    cap = slots // n_dp
    half = tok // 2
    pieces = feature_pieces(width)
    sec, dp, ten = lax.axis_index("section"), lax.axis_index("dp"), lax.axis_index("tensor")
    ring, core = ten // 2, ten % 2
    after = (sec + 1) % n_section
    before = (sec + n_section - 1) % n_section
    sends, takes = sec < n_section - 1, sec > 0
    sibling = (sec, dp, ring * 2 + 1 - core)
    right = (sec, dp, ((ring + 1) % n_ring) * 2 + core)
    left = (sec, dp, ((ring + n_ring - 1) % n_ring) * 2 + core)
    peers = [(sec, (dp + k) % n_dp, ten) for k in range(1, n_dp)]

    def remote(src, dst, sems, index, device, arrive=None):
        index = index if isinstance(index, tuple) else (index,)
        arrive = index if arrive is None else arrive
        return pltpu.make_async_remote_copy(
            src_ref=src,
            dst_ref=dst,
            send_sem=sems.at[(0, *index)],
            recv_sem=sems.at[(1, *arrive)],
            device_id=device,
            device_id_type=pl.DeviceIdType.MESH,
        )

    def shift(i):
        here = (slice(None), pl.ds(*pieces[i]))
        return remote(hidden.at[(0, 0, *here)], rows.at[here], shift_sem, i, (after, dp, ten))

    def send_meta():
        return remote(meta_out, meta_in, meta_sem, 0, (after, dp, ten))

    def send_ssq(k):
        return remote(ssq_out, ssq_in.at[ten], ssq_sem, k, (after, dp, k), (ten,))

    def take(i):
        pairs = [(owner, owner_vmem), (hidden.at[0, 0], own_rows), (gain, gain_vmem), (inverse, inverse_vmem)]
        pairs.append((weight.at[0], w_vmem))
        return pltpu.make_async_copy(*pairs[i], local_sem.at[i])

    barrier = pltpu.get_barrier_semaphore()

    def greet(devices):
        for device in devices:
            pl.semaphore_signal(
                barrier, inc=1, device_id=device, device_id_type=pl.DeviceIdType.MESH
            )

    @pl.when(takes)
    def _():
        greet([(before, dp, t) for t in range(n_tensor)])
        greet([sibling, right, left, *peers])

    @pl.when(sends)
    def _():
        take(0).start()
        take(1).start()

    @pl.when(takes)
    def _():
        for i in (2, 3, 4):
            take(i).start()

    @pl.when(sec == 0)
    def _():
        packed[...] = jnp.zeros_like(packed)
        pltpu.make_async_copy(packed, out.at[0, 0], keep_sem.at[0]).start()

    @pl.when(sends)
    def _():
        take(0).wait()
        row_id = lax.broadcasted_iota(I32, (8, tok), 0)
        meta_out[...] = jnp.where(
            row_id == 0, owner_vmem[...], jnp.where(row_id == 1, start[0, 0], live[0, 0])
        )

    within = 3 + len(peers)

    @pl.when(sends & takes)
    def _():
        pl.semaphore_wait(barrier, n_tensor + within)

    @pl.when(sec == 0)
    def _():
        pl.semaphore_wait(barrier, n_tensor)

    @pl.when(sec == n_section - 1)
    def _():
        pl.semaphore_wait(barrier, within)

    @pl.when(sends)
    def _():
        send_meta().start()
        shift(0).start()
        take(1).wait()
        squares = jnp.zeros((tok, HD), F32)
        for k in range(width // HD):
            piece = own_rows[:, k * HD : (k + 1) * HD].astype(F32)
            squares = squares + piece * piece
        ssq_out[...] = jnp.sum(squares.T, axis=0, keepdims=True)
        for k in range(n_tensor):
            send_ssq(k).start()
        for i in range(1, len(pieces)):
            shift(i).start()

    def prepare():
        send_meta().wait_recv()
        own_row = meta_in[0:1, :]
        alive = lax.broadcasted_iota(I32, (1, tok), 1) < meta_in[2:3, :]
        named = (lax.broadcasted_iota(I32, (16, tok), 0) == own_row) & alive
        named = jnp.where(named, 1.0, 0.0)
        row_at = lax.broadcasted_iota(I32, (tok, tok), 0)
        earlier = row_at < lax.broadcasted_iota(I32, (tok, tok), 1)
        ranks = dot(named.astype(BF16), jnp.where(earlier, 1.0, 0.0).astype(BF16))
        rank = jnp.sum(ranks * named, axis=0, keepdims=True).astype(I32)
        slot = jnp.where(alive, own_row * cap + rank, slots)
        placing = lax.broadcasted_iota(I32, (slots, tok), 0) == slot
        placing = jnp.where(placing, 1.0, 0.0).astype(BF16)
        place_ref[...] = placing
        position = lax.broadcasted_iota(I32, (tok, HD), 0) + meta_in[1:2, :HD]
        take(3).wait()
        take(2).wait()
        angle = position.astype(F32) * inverse_vmem[...]
        cos_ref[...] = jnp.cos(angle)
        front = lax.broadcasted_iota(I32, (tok, HD), 1) < HD // 2
        sine = jnp.sin(angle)
        sin_ref[...] = jnp.where(front, -sine, sine)
        for k in range(n_tensor):
            remote(ssq_out, ssq_in.at[k], ssq_sem, k, (after, dp, ten)).wait_recv()
        sum_sq = ssq_in[0]
        for k in range(1, n_tensor):
            sum_sq = sum_sq + ssq_in[k]
        scale = lax.rsqrt(sum_sq / d_model + EPSILON)
        scale_ref[...] = jnp.broadcast_to(scale, (HD, tok)).T

    def normed(at, wide):
        scale = scale_ref[...]
        parts = []
        for k in range(at, at + wide, HD):
            part = rows[:, k : k + HD].astype(F32) * gain_vmem[:, k : k + HD] * scale
            parts.append(part.astype(BF16))
        return jnp.concatenate(parts, axis=1)

    turns = (2, 1, n_ring - 1, 0)

    def chip(turn):
        return (ring + turn) % n_ring

    def cols_of(turn, side):
        return pl.ds(pl.multiple_of((chip(turn) * 2 + side) * columns, columns), columns)

    def pair(j):
        here = chip(turns[j])
        return remote(pair_out.at[here], pair_in.at[here], pair_sem, j, sibling)

    def project():
        for i, (at, wide) in enumerate(pieces[:-1]):
            shift(i).wait_recv()
            if i == 0:
                take(4).wait()
            activation = normed(at, wide)
            for n in range(0, total.shape[1], columns):
                cols = slice(n, n + columns)
                product = dot(activation, w_vmem[at : at + wide, cols])
                total[:, cols] = total[:, cols] + product if at else product
        at, wide = pieces[-1]
        shift(len(pieces) - 1).wait_recv()
        activation = normed(at, wide)
        for j, turn in enumerate(turns):
            cols = cols_of(turn, 1 - core)
            done = total[:, cols] + dot(activation, w_vmem[at : at + wide, cols])
            pair_out[chip(turn)] = done.astype(BF16)
            pair(j).start()
        for turn in turns:
            cols = cols_of(turn, core)
            total[:, cols] += dot(activation, w_vmem[at : at + wide, cols])

    def chip_sum(turn, rows_from, rows_to, cols):
        mine = total[rows_from:rows_to, cols_of(turn, core)]
        theirs = pair_in[chip(turn), rows_from:rows_to].astype(F32)
        return (mine + theirs)[:, cols]

    everything, key_cols, value_cols = slice(0, columns), slice(0, HD), slice(HD, columns)
    parts = (key_cols, value_cols)

    def hop(g, i, device):
        cols = everything if i < 2 else parts[g]
        here = (i, slice(None), pl.ds(cols.start, cols.stop - cols.start))
        return remote(hop_out.at[here], hop_in.at[here], hop_sem, (g, i), device)

    def straight(g):
        hop_out[2, :, parts[g]] = late_ref[2, :, parts[g]].astype(BF16)
        hop(g, 2, right).start()
        hop_out[3, :, parts[g]] = late_ref[3, :, parts[g]].astype(BF16)
        hop(g, 3, left).start()

    def relay(g):
        for side, device in ((0, right), (1, left)):
            if g == 0:
                hop(0, side, device).wait_recv()
            both = late_ref[side, :, parts[g]] + hop_in[side, :, parts[g]].astype(F32)
            hop_out[4 + side, :, parts[g]] = both.astype(BF16)
            hop(g, 4 + side, device).start()

    def ring_sums():
        pair(0).wait_recv()
        hop_out[0] = chip_sum(2, 0, half, everything).astype(BF16)
        hop(0, 0, right).start()
        hop_out[1] = chip_sum(2, half, tok, everything).astype(BF16)
        hop(0, 1, left).start()
        pair(1).wait_recv()
        late_ref[0] = chip_sum(1, 0, half, everything)
        late_ref[2] = chip_sum(1, half, tok, everything)
        pair(2).wait_recv()
        late_ref[1] = chip_sum(n_ring - 1, half, tok, everything)
        late_ref[3] = chip_sum(n_ring - 1, 0, half, everything)
        straight(0)
        relay(0)
        straight(1)
        relay(1)
        pair(3).wait_recv()

    def slot_rows(group):
        return pl.ds(pl.multiple_of(group * cap, 16), cap)

    def route(g, k):
        cols = pl.ds(g * HD, HD)
        peer = (dp + k) % n_dp
        return remote(
            packed.at[slot_rows(peer), cols],
            out.at[0, 0, slot_rows(dp), cols],
            route_sem,
            (g, k),
            (sec, peer, ten),
        )

    def keep(g):
        cols = pl.ds(g * HD, HD)
        return pltpu.make_async_copy(
            packed.at[slot_rows(dp), cols], out.at[0, 0, slot_rows(dp), cols], keep_sem.at[g]
        )

    routed = sorted(range(1, n_dp), key=lambda k: -min(k, n_dp - k))

    def finish(g):
        cols = parts[g]
        mine = chip_sum(0, 0, tok, cols)
        for i in (2, 3, 4, 5):
            hop(g, i, right).wait_recv()
        upper = hop_in[4, :, cols].astype(F32) + hop_in[3, :, cols].astype(F32)
        lower = hop_in[2, :, cols].astype(F32) + hop_in[5, :, cols].astype(F32)
        done = mine + jnp.concatenate([upper, lower], axis=0)
        if g == 0:
            done = done * cos_ref[...] + pltpu.roll(done, HD // 2, 1) * sin_ref[...]
        packed[:, cols] = dot(place_ref[...], done.astype(BF16)).astype(BF16)
        for k in routed:
            route(g, k).start()
        keep(g).start()

    @pl.when(takes)
    def _():
        prepare()
        project()
        ring_sums()
        finish(0)
        finish(1)
        for g in range(2):
            for k in routed:
                route(g, k).wait_recv()
        for g in range(2):
            for k in routed:
                route(g, k).wait_send()
            keep(g).wait()
            for i in range(2, 6):
                hop(g, i, right).wait_send()
        for j in range(len(turns)):
            pair(j).wait_send()
        hop(0, 0, right).wait_send()
        hop(0, 1, left).wait_send()

    @pl.when(sends)
    def _():
        for i in range(len(pieces)):
            shift(i).wait_send()
        send_meta().wait_send()
        for k in range(n_tensor):
            send_ssq(k).wait_send()

    @pl.when(sec == 0)
    def _():
        pltpu.make_async_copy(packed, out.at[0, 0], keep_sem.at[0]).wait()


def pinned(x):
    return pltpu.with_memory_space_constraint(x, pltpu.HBM)


def per_device(sizes, hidden, owner, start, live, norm_gain, w_kv):
    n_section, n_dp, n_tensor, d_model = sizes
    tok, width = hidden.shape[2:]
    columns = w_kv.shape[2]
    slots = (3 * tok // (2 * n_dp)) * n_dp
    local_cols = columns // n_tensor
    exponent = np.arange(HD // 2, dtype=np.float32) * np.float32(2.0) / np.float32(HD)
    inverse = np.power(np.float32(ROPE_BASE), -exponent).astype(np.float32)
    inverse = jnp.asarray(np.concatenate([inverse, inverse])[None, :])
    smem = pl.BlockSpec(memory_space=pltpu.SMEM)
    hbm = pl.BlockSpec(memory_space=pltpu.HBM)
    half = tok // 2
    n_ring = n_tensor // 2
    dma = pltpu.SemaphoreType.DMA
    return pl.pallas_call(
        functools.partial(kernel, sizes),
        out_shape=jax.ShapeDtypeStruct((1, 1, slots, local_cols), BF16),
        in_specs=[hbm, hbm, smem, smem, hbm, hbm, hbm],
        out_specs=hbm,
        scratch_shapes=[
            pltpu.VMEM((tok, width), BF16),
            pltpu.VMEM((1, tok), I32),
            pltpu.VMEM((1, width), F32),
            pltpu.VMEM((1, HD), F32),
            pltpu.VMEM((tok, width), BF16),
            pltpu.VMEM((width, columns), BF16),
            pltpu.VMEM((tok, columns), F32),
            pltpu.VMEM((1, tok), F32),
            pltpu.VMEM((n_tensor, 1, tok), F32),
            pltpu.VMEM((8, tok), I32),
            pltpu.VMEM((8, tok), I32),
            pltpu.VMEM((tok, HD), F32),
            pltpu.VMEM((tok, HD), F32),
            pltpu.VMEM((tok, HD), F32),
            pltpu.VMEM((slots, tok), BF16),
            pltpu.VMEM((n_ring, tok, local_cols), BF16),
            pltpu.VMEM((n_ring, tok, local_cols), BF16),
            pltpu.VMEM((6, half, local_cols), BF16),
            pltpu.VMEM((6, half, local_cols), BF16),
            pltpu.VMEM((4, half, local_cols), F32),
            pltpu.VMEM((slots, local_cols), BF16),
            dma((5,)),
            dma((2, len(feature_pieces(width)))),
            dma((2, n_tensor)),
            dma((2, 1)),
            dma((2, n_ring)),
            dma((2, 2, 6)),
            dma((2, 2, n_dp)),
            dma((2,)),
        ],
        compiler_params=pltpu.CompilerParams(
            collective_id=0, has_side_effects=True, vmem_limit_bytes=32 * 2**20
        ),
        cost_estimate=pl.CostEstimate(
            flops=2 * tok * width * columns,
            bytes_accessed=2 * width * (columns + 2 * tok),
            transcendentals=2 * tok * HD,
        ),
    )(pinned(hidden), pinned(owner.reshape(1, tok)), start, live, pinned(norm_gain), pinned(inverse), pinned(w_kv))


def solution(mesh):
    sizes = (mesh.shape["section"], mesh.shape["dp"], mesh.shape["tensor"])
    in_specs = (
        P("section", "dp", None, "tensor"),
        P("section", "dp", None, None),
        P("section", "dp"),
        P("section", "dp"),
        P("section", "tensor"),
        P("section", "tensor", None),
    )
    out_specs = P("section", "dp", None, "tensor")

    def run(hidden, owner, start, live, norm_gain, w_kv):
        body = functools.partial(per_device, (*sizes, hidden.shape[3]))
        return jax.shard_map(
            body, mesh=mesh, in_specs=in_specs, out_specs=out_specs, check_vma=False
        )(hidden, owner, start, live, norm_gain, w_kv)

    return run
```

```python
import functools

import jax
import jax.numpy as jnp
import numpy as np
from jax import lax
from jax.experimental import pallas as pl
from jax.experimental.pallas import tpu as pltpu
from jax.sharding import PartitionSpec as P

HD = 128
EPSILON = 1e-05
ROPE_BASE = 500000.0
F32 = jnp.float32
BF16 = jnp.bfloat16
I32 = jnp.int32


PIECES = 8


def feature_pieces(width):
    count = min(PIECES, width // HD)
    wide = width // count
    return [(i * wide, wide) for i in range(count)]


def dot(a, b):
    return jnp.dot(a, b, preferred_element_type=F32)


def kernel(
    sizes,
    hidden,
    owner,
    start,
    live,
    gain,
    inverse,
    weight,
    out,
    own_rows,
    owner_vmem,
    gain_vmem,
    inverse_vmem,
    rows,
    w_vmem,
    total,
    ssq_out,
    ssq_in,
    meta_out,
    meta_in,
    scale_ref,
    cos_ref,
    sin_ref,
    place_ref,
    pair_out,
    pair_in,
    hop_out,
    hop_in,
    late_ref,
    packed,
    local_sem,
    shift_sem,
    ssq_sem,
    meta_sem,
    pair_sem,
    hop_sem,
    route_sem,
    keep_sem,
):
    n_section, n_dp, n_tensor, d_model = sizes
    n_ring = n_tensor // 2
    tok, width = own_rows.shape
    slots, columns = packed.shape
    cap = slots // n_dp
    half = tok // 2
    pieces = feature_pieces(width)
    sec, dp, ten = lax.axis_index("section"), lax.axis_index("dp"), lax.axis_index("tensor")
    ring, core = ten // 2, ten % 2
    after = (sec + 1) % n_section
    before = (sec + n_section - 1) % n_section
    sends, takes = sec < n_section - 1, sec > 0
    sibling = (sec, dp, ring * 2 + 1 - core)
    right = (sec, dp, ((ring + 1) % n_ring) * 2 + core)
    left = (sec, dp, ((ring + n_ring - 1) % n_ring) * 2 + core)
    peers = [(sec, (dp + k) % n_dp, ten) for k in range(1, n_dp)]

    def remote(src, dst, sems, index, device, arrive=None):
        index = index if isinstance(index, tuple) else (index,)
        arrive = index if arrive is None else arrive
        return pltpu.make_async_remote_copy(
            src_ref=src,
            dst_ref=dst,
            send_sem=sems.at[(0, *index)],
            recv_sem=sems.at[(1, *arrive)],
            device_id=device,
            device_id_type=pl.DeviceIdType.MESH,
        )

    def shift(i):
        here = (slice(None), pl.ds(*pieces[i]))
        return remote(hidden.at[(0, 0, *here)], rows.at[here], shift_sem, i, (after, dp, ten))

    def send_meta():
        return remote(meta_out, meta_in, meta_sem, 0, (after, dp, ten))

    def send_ssq(k):
        return remote(ssq_out, ssq_in.at[ten], ssq_sem, k, (after, dp, k), (ten,))

    def take(i):
        pairs = [(owner, owner_vmem), (hidden.at[0, 0], own_rows), (gain, gain_vmem), (inverse, inverse_vmem)]
        pairs.append((weight.at[0], w_vmem))
        return pltpu.make_async_copy(*pairs[i], local_sem.at[i])

    barrier = pltpu.get_barrier_semaphore()

    def greet(devices):
        for device in devices:
            pl.semaphore_signal(
                barrier, inc=1, device_id=device, device_id_type=pl.DeviceIdType.MESH
            )

    @pl.when(takes)
    def _():
        greet([(before, dp, t) for t in range(n_tensor)])
        greet([sibling, right, left, *peers])

    @pl.when(sends)
    def _():
        take(0).start()
        take(1).start()

    @pl.when(takes)
    def _():
        for i in (2, 3, 4):
            take(i).start()

    @pl.when(sec == 0)
    def _():
        packed[...] = jnp.zeros_like(packed)
        pltpu.make_async_copy(packed, out.at[0, 0], keep_sem.at[0]).start()

    @pl.when(sends)
    def _():
        take(0).wait()
        row_id = lax.broadcasted_iota(I32, (8, tok), 0)
        meta_out[...] = jnp.where(
            row_id == 0, owner_vmem[...], jnp.where(row_id == 1, start[0, 0], live[0, 0])
        )

    within = 3 + len(peers)

    @pl.when(sends & takes)
    def _():
        pl.semaphore_wait(barrier, n_tensor + within)

    @pl.when(sec == 0)
    def _():
        pl.semaphore_wait(barrier, n_tensor)

    @pl.when(sec == n_section - 1)
    def _():
        pl.semaphore_wait(barrier, within)

    @pl.when(sends)
    def _():
        send_meta().start()
        shift(0).start()
        take(1).wait()
        squares = jnp.zeros((tok, HD), F32)
        for k in range(width // HD):
            piece = own_rows[:, k * HD : (k + 1) * HD].astype(F32)
            squares = squares + piece * piece
        ssq_out[...] = jnp.sum(squares.T, axis=0, keepdims=True)
        for k in range(n_tensor):
            send_ssq(k).start()
        for i in range(1, len(pieces)):
            shift(i).start()

    def prepare():
        send_meta().wait_recv()
        own_row = meta_in[0:1, :]
        alive = lax.broadcasted_iota(I32, (1, tok), 1) < meta_in[2:3, :]
        named = (lax.broadcasted_iota(I32, (16, tok), 0) == own_row) & alive
        named = jnp.where(named, 1.0, 0.0)
        row_at = lax.broadcasted_iota(I32, (tok, tok), 0)
        earlier = row_at < lax.broadcasted_iota(I32, (tok, tok), 1)
        ranks = dot(named.astype(BF16), jnp.where(earlier, 1.0, 0.0).astype(BF16))
        rank = jnp.sum(ranks * named, axis=0, keepdims=True).astype(I32)
        slot = jnp.where(alive, own_row * cap + rank, slots)
        placing = lax.broadcasted_iota(I32, (slots, tok), 0) == slot
        placing = jnp.where(placing, 1.0, 0.0).astype(BF16)
        place_ref[...] = placing
        position = lax.broadcasted_iota(I32, (tok, HD), 0) + meta_in[1:2, :HD]
        take(3).wait()
        take(2).wait()
        angle = position.astype(F32) * inverse_vmem[...]
        cos_ref[...] = jnp.cos(angle)
        front = lax.broadcasted_iota(I32, (tok, HD), 1) < HD // 2
        sine = jnp.sin(angle)
        sin_ref[...] = jnp.where(front, -sine, sine)
        for k in range(n_tensor):
            remote(ssq_out, ssq_in.at[k], ssq_sem, k, (after, dp, ten)).wait_recv()
        sum_sq = ssq_in[0]
        for k in range(1, n_tensor):
            sum_sq = sum_sq + ssq_in[k]
        scale = lax.rsqrt(sum_sq / d_model + EPSILON)
        scale_ref[...] = jnp.broadcast_to(scale, (HD, tok)).T

    def normed(at, wide):
        scale = scale_ref[...]
        parts = []
        for k in range(at, at + wide, HD):
            part = rows[:, k : k + HD].astype(F32) * gain_vmem[:, k : k + HD] * scale
            parts.append(part.astype(BF16))
        return jnp.concatenate(parts, axis=1)

    turns = (2, 1, n_ring - 1, 0)

    def chip(turn):
        return (ring + turn) % n_ring

    def cols_of(turn, side):
        return pl.ds(pl.multiple_of((chip(turn) * 2 + side) * columns, columns), columns)

    def pair(j):
        here = chip(turns[j])
        return remote(pair_out.at[here], pair_in.at[here], pair_sem, j, sibling)

    def project():
        for i, (at, wide) in enumerate(pieces[:-1]):
            shift(i).wait_recv()
            if i == 0:
                take(4).wait()
            activation = normed(at, wide)
            for n in range(0, total.shape[1], columns):
                cols = slice(n, n + columns)
                product = dot(activation, w_vmem[at : at + wide, cols])
                total[:, cols] = total[:, cols] + product if at else product
        at, wide = pieces[-1]
        shift(len(pieces) - 1).wait_recv()
        activation = normed(at, wide)
        for j, turn in enumerate(turns):
            cols = cols_of(turn, 1 - core)
            done = total[:, cols] + dot(activation, w_vmem[at : at + wide, cols])
            pair_out[chip(turn)] = done.astype(BF16)
            pair(j).start()
        for turn in turns:
            cols = cols_of(turn, core)
            total[:, cols] += dot(activation, w_vmem[at : at + wide, cols])

    def chip_sum(turn, rows_from, rows_to, cols):
        mine = total[rows_from:rows_to, cols_of(turn, core)]
        theirs = pair_in[chip(turn), rows_from:rows_to].astype(F32)
        return (mine + theirs)[:, cols]

    everything, key_cols, value_cols = slice(0, columns), slice(0, HD), slice(HD, columns)
    parts = (key_cols, value_cols)

    def hop(g, i, device):
        here = (i, slice(None), pl.ds(parts[g].start, HD))
        return remote(hop_out.at[here], hop_in.at[here], hop_sem, (g, i), device)

    def straight(g):
        hop_out[2, :, parts[g]] = late_ref[2, :, parts[g]].astype(BF16)
        hop(g, 2, right).start()
        hop_out[3, :, parts[g]] = late_ref[3, :, parts[g]].astype(BF16)
        hop(g, 3, left).start()

    def relay(g):
        for side, device in ((0, right), (1, left)):
            hop(g, side, device).wait_recv()
            both = late_ref[side, :, parts[g]] + hop_in[side, :, parts[g]].astype(F32)
            hop_out[4 + side, :, parts[g]] = both.astype(BF16)
            hop(g, 4 + side, device).start()

    def ring_sums():
        pair(0).wait_recv()
        hop_out[0] = chip_sum(2, 0, half, everything).astype(BF16)
        hop(0, 0, right).start()
        hop_out[1] = chip_sum(2, half, tok, everything).astype(BF16)
        hop(0, 1, left).start()
        pair(1).wait_recv()
        late_ref[0] = chip_sum(1, 0, half, everything)
        late_ref[2] = chip_sum(1, half, tok, everything)
        pair(2).wait_recv()
        late_ref[1] = chip_sum(n_ring - 1, half, tok, everything)
        late_ref[3] = chip_sum(n_ring - 1, 0, half, everything)
        straight(0)
        hop(1, 0, right).start()
        hop(1, 1, left).start()
        relay(0)
        straight(1)
        relay(1)
        pair(3).wait_recv()

    def slot_rows(group):
        return pl.ds(pl.multiple_of(group * cap, 16), cap)

    def route(g, k):
        cols = pl.ds(g * HD, HD)
        peer = (dp + k) % n_dp
        return remote(
            packed.at[slot_rows(peer), cols],
            out.at[0, 0, slot_rows(dp), cols],
            route_sem,
            (g, k),
            (sec, peer, ten),
        )

    def keep(g):
        cols = pl.ds(g * HD, HD)
        return pltpu.make_async_copy(
            packed.at[slot_rows(dp), cols], out.at[0, 0, slot_rows(dp), cols], keep_sem.at[g]
        )

    routed = sorted(range(1, n_dp), key=lambda k: -min(k, n_dp - k))

    def finish(g):
        cols = parts[g]
        hop(g, 2, right).wait_recv()
        lower = chip_sum(0, half, tok, cols) + hop_in[2, :, cols].astype(F32)
        hop(g, 3, left).wait_recv()
        upper = chip_sum(0, 0, half, cols) + hop_in[3, :, cols].astype(F32)
        hop(g, 4, right).wait_recv()
        upper = upper + hop_in[4, :, cols].astype(F32)
        hop(g, 5, left).wait_recv()
        lower = lower + hop_in[5, :, cols].astype(F32)
        done = jnp.concatenate([upper, lower], axis=0)
        if g == 0:
            done = done * cos_ref[...] + pltpu.roll(done, HD // 2, 1) * sin_ref[...]
        packed[:, cols] = dot(place_ref[...], done.astype(BF16)).astype(BF16)
        for k in routed:
            route(g, k).start()
        keep(g).start()

    @pl.when(takes)
    def _():
        prepare()
        project()
        ring_sums()
        finish(0)
        finish(1)
        for g in range(2):
            for k in routed:
                route(g, k).wait_recv()
        for g in range(2):
            for k in routed:
                route(g, k).wait_send()
            keep(g).wait()
            for i in range(6):
                hop(g, i, right).wait_send()
        for j in range(len(turns)):
            pair(j).wait_send()

    @pl.when(sends)
    def _():
        for i in range(len(pieces)):
            shift(i).wait_send()
        send_meta().wait_send()
        for k in range(n_tensor):
            send_ssq(k).wait_send()

    @pl.when(sec == 0)
    def _():
        pltpu.make_async_copy(packed, out.at[0, 0], keep_sem.at[0]).wait()


def pinned(x):
    return pltpu.with_memory_space_constraint(x, pltpu.HBM)


def per_device(sizes, hidden, owner, start, live, norm_gain, w_kv):
    n_section, n_dp, n_tensor, d_model = sizes
    tok, width = hidden.shape[2:]
    columns = w_kv.shape[2]
    slots = (3 * tok // (2 * n_dp)) * n_dp
    local_cols = columns // n_tensor
    exponent = np.arange(HD // 2, dtype=np.float32) * np.float32(2.0) / np.float32(HD)
    inverse = np.power(np.float32(ROPE_BASE), -exponent).astype(np.float32)
    inverse = jnp.asarray(np.concatenate([inverse, inverse])[None, :])
    smem = pl.BlockSpec(memory_space=pltpu.SMEM)
    hbm = pl.BlockSpec(memory_space=pltpu.HBM)
    half = tok // 2
    n_ring = n_tensor // 2
    dma = pltpu.SemaphoreType.DMA
    return pl.pallas_call(
        functools.partial(kernel, sizes),
        out_shape=jax.ShapeDtypeStruct((1, 1, slots, local_cols), BF16),
        in_specs=[hbm, hbm, smem, smem, hbm, hbm, hbm],
        out_specs=hbm,
        scratch_shapes=[
            pltpu.VMEM((tok, width), BF16),
            pltpu.VMEM((1, tok), I32),
            pltpu.VMEM((1, width), F32),
            pltpu.VMEM((1, HD), F32),
            pltpu.VMEM((tok, width), BF16),
            pltpu.VMEM((width, columns), BF16),
            pltpu.VMEM((tok, columns), F32),
            pltpu.VMEM((1, tok), F32),
            pltpu.VMEM((n_tensor, 1, tok), F32),
            pltpu.VMEM((8, tok), I32),
            pltpu.VMEM((8, tok), I32),
            pltpu.VMEM((tok, HD), F32),
            pltpu.VMEM((tok, HD), F32),
            pltpu.VMEM((tok, HD), F32),
            pltpu.VMEM((slots, tok), BF16),
            pltpu.VMEM((n_ring, tok, local_cols), BF16),
            pltpu.VMEM((n_ring, tok, local_cols), BF16),
            pltpu.VMEM((6, half, local_cols), BF16),
            pltpu.VMEM((6, half, local_cols), BF16),
            pltpu.VMEM((4, half, local_cols), F32),
            pltpu.VMEM((slots, local_cols), BF16),
            dma((5,)),
            dma((2, len(feature_pieces(width)))),
            dma((2, n_tensor)),
            dma((2, 1)),
            dma((2, n_ring)),
            dma((2, 2, 6)),
            dma((2, 2, n_dp)),
            dma((2,)),
        ],
        compiler_params=pltpu.CompilerParams(
            collective_id=0, has_side_effects=True, vmem_limit_bytes=32 * 2**20
        ),
        cost_estimate=pl.CostEstimate(
            flops=2 * tok * width * columns,
            bytes_accessed=2 * width * (columns + 2 * tok),
            transcendentals=2 * tok * HD,
        ),
    )(pinned(hidden), pinned(owner.reshape(1, tok)), start, live, pinned(norm_gain), pinned(inverse), pinned(w_kv))


def solution(mesh):
    sizes = (mesh.shape["section"], mesh.shape["dp"], mesh.shape["tensor"])
    in_specs = (
        P("section", "dp", None, "tensor"),
        P("section", "dp", None, None),
        P("section", "dp"),
        P("section", "dp"),
        P("section", "tensor"),
        P("section", "tensor", None),
    )
    out_specs = P("section", "dp", None, "tensor")

    def run(hidden, owner, start, live, norm_gain, w_kv):
        body = functools.partial(per_device, (*sizes, hidden.shape[3]))
        return jax.shard_map(
            body, mesh=mesh, in_specs=in_specs, out_specs=out_specs, check_vma=False
        )(hidden, owner, start, live, norm_gain, w_kv)

    return run
```

```python
import functools

import jax
import jax.numpy as jnp
import numpy as np
from jax import lax
from jax.experimental import pallas as pl
from jax.experimental.pallas import tpu as pltpu
from jax.sharding import PartitionSpec as P

HD = 128
EPSILON = 1e-05
ROPE_BASE = 500000.0
F32 = jnp.float32
BF16 = jnp.bfloat16
I32 = jnp.int32


PIECES = 8


def feature_pieces(width):
    count = min(PIECES, width // HD)
    wide = width // count
    return [(i * wide, wide) for i in range(count)]


def dot(a, b):
    return jnp.dot(a, b, preferred_element_type=F32)


def kernel(
    sizes,
    hidden,
    owner,
    start,
    live,
    gain,
    inverse,
    weight,
    out,
    own_rows,
    owner_vmem,
    gain_vmem,
    inverse_vmem,
    rows,
    w_vmem,
    total,
    ssq_out,
    ssq_in,
    meta_out,
    meta_in,
    scale_ref,
    cos_ref,
    sin_ref,
    place_ref,
    pair_out,
    pair_in,
    hop_out,
    hop_in,
    late_ref,
    packed,
    local_sem,
    shift_sem,
    ssq_sem,
    meta_sem,
    pair_sem,
    hop_sem,
    route_sem,
    keep_sem,
):
    n_section, n_dp, n_tensor, d_model = sizes
    n_ring = n_tensor // 2
    tok, width = own_rows.shape
    slots, columns = packed.shape
    cap = slots // n_dp
    half = tok // 2
    pieces = feature_pieces(width)
    sec, dp, ten = lax.axis_index("section"), lax.axis_index("dp"), lax.axis_index("tensor")
    ring, core = ten // 2, ten % 2
    after = (sec + 1) % n_section
    before = (sec + n_section - 1) % n_section
    sends, takes = sec < n_section - 1, sec > 0
    sibling = (sec, dp, ring * 2 + 1 - core)
    right = (sec, dp, ((ring + 1) % n_ring) * 2 + core)
    left = (sec, dp, ((ring + n_ring - 1) % n_ring) * 2 + core)
    peers = [(sec, (dp + k) % n_dp, ten) for k in range(1, n_dp)]

    def remote(src, dst, sems, index, device, arrive=None):
        index = index if isinstance(index, tuple) else (index,)
        arrive = index if arrive is None else arrive
        return pltpu.make_async_remote_copy(
            src_ref=src,
            dst_ref=dst,
            send_sem=sems.at[(0, *index)],
            recv_sem=sems.at[(1, *arrive)],
            device_id=device,
            device_id_type=pl.DeviceIdType.MESH,
        )

    def shift(i):
        here = (slice(None), pl.ds(*pieces[i]))
        return remote(hidden.at[(0, 0, *here)], rows.at[here], shift_sem, i, (after, dp, ten))

    def send_meta():
        return remote(meta_out, meta_in, meta_sem, 0, (after, dp, ten))

    def send_ssq(k):
        return remote(ssq_out, ssq_in.at[ten], ssq_sem, k, (after, dp, k), (ten,))

    def take(i):
        pairs = [(owner, owner_vmem), (hidden.at[0, 0], own_rows), (gain, gain_vmem), (inverse, inverse_vmem)]
        pairs.append((weight.at[0], w_vmem))
        return pltpu.make_async_copy(*pairs[i], local_sem.at[i])

    barrier = pltpu.get_barrier_semaphore()

    def greet(devices):
        for device in devices:
            pl.semaphore_signal(
                barrier, inc=1, device_id=device, device_id_type=pl.DeviceIdType.MESH
            )

    @pl.when(takes)
    def _():
        greet([(before, dp, t) for t in range(n_tensor)])
        greet([sibling, right, left, *peers])

    @pl.when(sends)
    def _():
        take(0).start()
        take(1).start()

    @pl.when(takes)
    def _():
        for i in (2, 3, 4):
            take(i).start()

    @pl.when(sec == 0)
    def _():
        packed[...] = jnp.zeros_like(packed)
        pltpu.make_async_copy(packed, out.at[0, 0], keep_sem.at[0]).start()

    @pl.when(sends)
    def _():
        take(0).wait()
        row_id = lax.broadcasted_iota(I32, (8, tok), 0)
        meta_out[...] = jnp.where(
            row_id == 0, owner_vmem[...], jnp.where(row_id == 1, start[0, 0], live[0, 0])
        )

    within = 3 + len(peers)

    @pl.when(sends & takes)
    def _():
        pl.semaphore_wait(barrier, n_tensor + within)

    @pl.when(sec == 0)
    def _():
        pl.semaphore_wait(barrier, n_tensor)

    @pl.when(sec == n_section - 1)
    def _():
        pl.semaphore_wait(barrier, within)

    @pl.when(sends)
    def _():
        send_meta().start()
        shift(0).start()
        shift(1).start()
        take(1).wait()
        squares = jnp.zeros((tok, HD), F32)
        for k in range(width // HD):
            piece = own_rows[:, k * HD : (k + 1) * HD].astype(F32)
            squares = squares + piece * piece
        ssq_out[...] = jnp.sum(squares.T, axis=0, keepdims=True)
        for k in range(n_tensor):
            send_ssq(k).start()
        for i in range(2, len(pieces)):
            shift(i).start()

    def prepare():
        send_meta().wait_recv()
        own_row = meta_in[0:1, :]
        alive = lax.broadcasted_iota(I32, (1, tok), 1) < meta_in[2:3, :]
        named = (lax.broadcasted_iota(I32, (16, tok), 0) == own_row) & alive
        named = jnp.where(named, 1.0, 0.0)
        row_at = lax.broadcasted_iota(I32, (tok, tok), 0)
        earlier = row_at < lax.broadcasted_iota(I32, (tok, tok), 1)
        ranks = dot(named.astype(BF16), jnp.where(earlier, 1.0, 0.0).astype(BF16))
        rank = jnp.sum(ranks * named, axis=0, keepdims=True).astype(I32)
        slot = jnp.where(alive, own_row * cap + rank, slots)
        placing = lax.broadcasted_iota(I32, (slots, tok), 0) == slot
        placing = jnp.where(placing, 1.0, 0.0).astype(BF16)
        place_ref[...] = placing
        position = lax.broadcasted_iota(I32, (tok, HD), 0) + meta_in[1:2, :HD]
        take(3).wait()
        take(2).wait()
        angle = position.astype(F32) * inverse_vmem[...]
        cos_ref[...] = jnp.cos(angle)
        front = lax.broadcasted_iota(I32, (tok, HD), 1) < HD // 2
        sine = jnp.sin(angle)
        sin_ref[...] = jnp.where(front, -sine, sine)
        for k in range(n_tensor):
            remote(ssq_out, ssq_in.at[k], ssq_sem, k, (after, dp, ten)).wait_recv()
        sum_sq = ssq_in[0]
        for k in range(1, n_tensor):
            sum_sq = sum_sq + ssq_in[k]
        scale = lax.rsqrt(sum_sq / d_model + EPSILON)
        scale_ref[...] = jnp.broadcast_to(scale, (HD, tok)).T

    def normed(at, wide):
        scale = scale_ref[...]
        parts = []
        for k in range(at, at + wide, HD):
            part = rows[:, k : k + HD].astype(F32) * gain_vmem[:, k : k + HD] * scale
            parts.append(part.astype(BF16))
        return jnp.concatenate(parts, axis=1)

    turns = (2, 1, n_ring - 1, 0)

    def chip(turn):
        return (ring + turn) % n_ring

    def cols_of(turn, side):
        return pl.ds(pl.multiple_of((chip(turn) * 2 + side) * columns, columns), columns)

    def pair(j):
        here = chip(turns[j])
        return remote(pair_out.at[here], pair_in.at[here], pair_sem, j, sibling)

    def project():
        for i, (at, wide) in enumerate(pieces[:-1]):
            shift(i).wait_recv()
            if i == 0:
                take(4).wait()
            activation = normed(at, wide)
            for n in range(0, total.shape[1], columns):
                cols = slice(n, n + columns)
                product = dot(activation, w_vmem[at : at + wide, cols])
                total[:, cols] = total[:, cols] + product if at else product
        at, wide = pieces[-1]
        shift(len(pieces) - 1).wait_recv()
        activation = normed(at, wide)
        for j, turn in enumerate(turns):
            if j == 2:
                far_sums()
            cols = cols_of(turn, 1 - core)
            done = total[:, cols] + dot(activation, w_vmem[at : at + wide, cols])
            pair_out[chip(turn)] = done.astype(BF16)
            pair(j).start()
            cols = cols_of(turn, core)
            total[:, cols] += dot(activation, w_vmem[at : at + wide, cols])

    def chip_sum(turn, rows_from, rows_to, cols):
        mine = total[rows_from:rows_to, cols_of(turn, core)]
        theirs = pair_in[chip(turn), rows_from:rows_to].astype(F32)
        return (mine + theirs)[:, cols]

    everything, key_cols, value_cols = slice(0, columns), slice(0, HD), slice(HD, columns)
    parts = (key_cols, value_cols)

    def hop(g, i, device):
        here = (i, slice(None), pl.ds(parts[g].start, HD))
        return remote(hop_out.at[here], hop_in.at[here], hop_sem, (g, i), device)

    def straight(g):
        hop_out[2, :, parts[g]] = late_ref[2, :, parts[g]].astype(BF16)
        hop(g, 2, right).start()
        hop_out[3, :, parts[g]] = late_ref[3, :, parts[g]].astype(BF16)
        hop(g, 3, left).start()

    def relay(g):
        for side, device in ((0, right), (1, left)):
            hop(g, side, device).wait_recv()
            both = late_ref[side, :, parts[g]] + hop_in[side, :, parts[g]].astype(F32)
            hop_out[4 + side, :, parts[g]] = both.astype(BF16)
            hop(g, 4 + side, device).start()

    def far_sums():
        pair(0).wait_recv()
        hop_out[0] = chip_sum(2, 0, half, everything).astype(BF16)
        hop(0, 0, right).start()
        hop_out[1] = chip_sum(2, half, tok, everything).astype(BF16)
        hop(0, 1, left).start()

    def ring_sums():
        pair(1).wait_recv()
        late_ref[0] = chip_sum(1, 0, half, everything)
        late_ref[2] = chip_sum(1, half, tok, everything)
        pair(2).wait_recv()
        late_ref[1] = chip_sum(n_ring - 1, half, tok, everything)
        late_ref[3] = chip_sum(n_ring - 1, 0, half, everything)
        straight(0)
        hop(1, 0, right).start()
        hop(1, 1, left).start()
        relay(0)
        straight(1)
        relay(1)
        pair(3).wait_recv()

    def slot_rows(group):
        return pl.ds(pl.multiple_of(group * cap, 16), cap)

    def route(g, k):
        cols = pl.ds(g * HD, HD)
        peer = (dp + k) % n_dp
        return remote(
            packed.at[slot_rows(peer), cols],
            out.at[0, 0, slot_rows(dp), cols],
            route_sem,
            (g, k),
            (sec, peer, ten),
        )

    def keep(g):
        cols = pl.ds(g * HD, HD)
        return pltpu.make_async_copy(
            packed.at[slot_rows(dp), cols], out.at[0, 0, slot_rows(dp), cols], keep_sem.at[g]
        )

    routed = sorted(range(1, n_dp), key=lambda k: -min(k, n_dp - k))

    def finish(g):
        cols = parts[g]
        hop(g, 2, right).wait_recv()
        lower = chip_sum(0, half, tok, cols) + hop_in[2, :, cols].astype(F32)
        hop(g, 3, left).wait_recv()
        upper = chip_sum(0, 0, half, cols) + hop_in[3, :, cols].astype(F32)
        hop(g, 4, right).wait_recv()
        upper = upper + hop_in[4, :, cols].astype(F32)
        hop(g, 5, left).wait_recv()
        lower = lower + hop_in[5, :, cols].astype(F32)
        done = jnp.concatenate([upper, lower], axis=0)
        if g == 0:
            done = done * cos_ref[...] + pltpu.roll(done, HD // 2, 1) * sin_ref[...]
        packed[:, cols] = dot(place_ref[...], done.astype(BF16)).astype(BF16)
        for k in routed:
            route(g, k).start()
        keep(g).start()

    @pl.when(takes)
    def _():
        prepare()
        project()
        ring_sums()
        finish(0)
        finish(1)
        for g in range(2):
            for k in routed:
                route(g, k).wait_recv()
        for g in range(2):
            for k in routed:
                route(g, k).wait_send()
            keep(g).wait()
            for i in range(6):
                hop(g, i, right).wait_send()
        for j in range(len(turns)):
            pair(j).wait_send()

    @pl.when(sends)
    def _():
        for i in range(len(pieces)):
            shift(i).wait_send()
        send_meta().wait_send()
        for k in range(n_tensor):
            send_ssq(k).wait_send()

    @pl.when(sec == 0)
    def _():
        pltpu.make_async_copy(packed, out.at[0, 0], keep_sem.at[0]).wait()


def pinned(x):
    return pltpu.with_memory_space_constraint(x, pltpu.HBM)


def per_device(sizes, hidden, owner, start, live, norm_gain, w_kv):
    n_section, n_dp, n_tensor, d_model = sizes
    tok, width = hidden.shape[2:]
    columns = w_kv.shape[2]
    slots = (3 * tok // (2 * n_dp)) * n_dp
    local_cols = columns // n_tensor
    exponent = np.arange(HD // 2, dtype=np.float32) * np.float32(2.0) / np.float32(HD)
    inverse = np.power(np.float32(ROPE_BASE), -exponent).astype(np.float32)
    inverse = jnp.asarray(np.concatenate([inverse, inverse])[None, :])
    smem = pl.BlockSpec(memory_space=pltpu.SMEM)
    hbm = pl.BlockSpec(memory_space=pltpu.HBM)
    half = tok // 2
    n_ring = n_tensor // 2
    dma = pltpu.SemaphoreType.DMA
    return pl.pallas_call(
        functools.partial(kernel, sizes),
        out_shape=jax.ShapeDtypeStruct((1, 1, slots, local_cols), BF16),
        in_specs=[hbm, hbm, smem, smem, hbm, hbm, hbm],
        out_specs=hbm,
        scratch_shapes=[
            pltpu.VMEM((tok, width), BF16),
            pltpu.VMEM((1, tok), I32),
            pltpu.VMEM((1, width), F32),
            pltpu.VMEM((1, HD), F32),
            pltpu.VMEM((tok, width), BF16),
            pltpu.VMEM((width, columns), BF16),
            pltpu.VMEM((tok, columns), F32),
            pltpu.VMEM((1, tok), F32),
            pltpu.VMEM((n_tensor, 1, tok), F32),
            pltpu.VMEM((8, tok), I32),
            pltpu.VMEM((8, tok), I32),
            pltpu.VMEM((tok, HD), F32),
            pltpu.VMEM((tok, HD), F32),
            pltpu.VMEM((tok, HD), F32),
            pltpu.VMEM((slots, tok), BF16),
            pltpu.VMEM((n_ring, tok, local_cols), BF16),
            pltpu.VMEM((n_ring, tok, local_cols), BF16),
            pltpu.VMEM((6, half, local_cols), BF16),
            pltpu.VMEM((6, half, local_cols), BF16),
            pltpu.VMEM((4, half, local_cols), F32),
            pltpu.VMEM((slots, local_cols), BF16),
            dma((5,)),
            dma((2, len(feature_pieces(width)))),
            dma((2, n_tensor)),
            dma((2, 1)),
            dma((2, n_ring)),
            dma((2, 2, 6)),
            dma((2, 2, n_dp)),
            dma((2,)),
        ],
        compiler_params=pltpu.CompilerParams(
            collective_id=0, has_side_effects=True, vmem_limit_bytes=32 * 2**20
        ),
        cost_estimate=pl.CostEstimate(
            flops=2 * tok * width * columns,
            bytes_accessed=2 * width * (columns + 2 * tok),
            transcendentals=2 * tok * HD,
        ),
    )(pinned(hidden), pinned(owner.reshape(1, tok)), start, live, pinned(norm_gain), pinned(inverse), pinned(w_kv))


def solution(mesh):
    sizes = (mesh.shape["section"], mesh.shape["dp"], mesh.shape["tensor"])
    in_specs = (
        P("section", "dp", None, "tensor"),
        P("section", "dp", None, None),
        P("section", "dp"),
        P("section", "dp"),
        P("section", "tensor"),
        P("section", "tensor", None),
    )
    out_specs = P("section", "dp", None, "tensor")

    def run(hidden, owner, start, live, norm_gain, w_kv):
        body = functools.partial(per_device, (*sizes, hidden.shape[3]))
        return jax.shard_map(
            body, mesh=mesh, in_specs=in_specs, out_specs=out_specs, check_vma=False
        )(hidden, owner, start, live, norm_gain, w_kv)

    return run
```
